512 devices in a mesh: row: 32 (over y, z_lo), col: 16 (over x, z_hi, core).
Axes of the slice: x: 4, y: 4, z: 16 (z_hi: 2, z_lo: 8; z = z_hi * 8 + z_lo), core: 2. Of those that a mesh axis runs over, the one named last changes fastest.
Arguments:
- cotangent: bfloat16 [16, 256, 256], P('col', 'row'), may hold values from -0.125 to 0.125
- preact_two: bfloat16 [16, 256, 256], P('col', 'row'), may hold values from -6 to 6
- aggregate_two: bfloat16 [16, 256, 256], P('col', 'row'), may hold values from 0 to 2
- self_hidden: bfloat16 [16, 256, 256], P('col', 'row'), may hold values from 0 to 2
- neigh_weight: bfloat16 [256, 256], replicated, may hold values from -0.375 to 0.375
- root_weight: bfloat16 [256, 256], replicated, may hold values from -0.375 to 0.375
- sampled_tiles: bfloat16 [32, 16, 16, 128, 128], P('row', 'col'), may hold values from 0 to 0.049804688
- tile_slot: int32 [32, 16, 16], P('row', 'col'), may hold values from 0 to 31, as said below
- tile_count: int32 [32, 16], P('row', 'col'), may hold values from 1 to 16, as said below
- target_self: int32 [16, 256], P('col'), may hold values from 0 to 65535, as said below
- preact_one: bfloat16 [32, 2048, 256], P('row', 'col'), may hold values from -6 to 6
- aggregate_one: bfloat16 [32, 2048, 768], P('row', 'col'), may hold values from -6 to 6
- feature_one: bfloat16 [32, 2048, 768], P('row', 'col'), may hold values from -6 to 6
Outputs:
- layer_two_grads: float32 [2, 256, 256], replicated
- layer_one_grads: float32 [2, 768, 256], replicated
The draws below stay inside these ranges and needn't reach their ends.
Inputs may be any that keep to these rules, and one draw needn't show every extreme that they name: `tile_slot`: within one block the 16 slots hold distinct positions; position s is tile row s // 16 and tile column s % 16 of the block. `tile_count`: slots from a block's count on hold no tile. Some block is full in every draw. `target_self`: all values are distinct.
All inputs are finite; a program needn't handle non-finite values.
Results may differ from the reference program's by a relative error of at most 0.013.
Values may be sent and summed in bfloat16 or wider, within the bound.
No kernel may reach another device: no remote copies, remote signals or barrier semaphores. Data moves between devices by JAX's collectives and lax.ppermute only.
A program may use at most 64 MiB of HBM per device.

```python
import jax
import jax.numpy as jnp
from jax import lax

FEAT = 768
HID = 256
TILE = 128
DST_TILES = 2
SRC_TILES = 16
DST_BLOCK = 256
SRC_BLOCK = 2048
TILE_CAP = 16
DST_NODES = 4096
SRC_NODES = 65536
N_ROW = 32
N_COL = 16


def draw_tile_slot(key, part):
    key = jax.random.fold_in(key, 11)
    device_keys = jax.random.split(key, N_ROW * N_COL)
    chosen = jax.vmap(lambda one_key: jax.random.permutation(one_key, DST_TILES * SRC_TILES)[:TILE_CAP])(device_keys)
    return chosen.reshape(N_ROW, N_COL, TILE_CAP).astype(jnp.int32)


def draw_tile_count(key, part):
    key = jax.random.fold_in(key, 23)
    key_one, key_two, key_full = jax.random.split(key, 3)
    factor_one = jax.random.randint(key_one, (N_ROW * N_COL,), 0, TILE_CAP)
    factor_two = jax.random.randint(key_two, (N_ROW * N_COL,), 0, TILE_CAP + 1)
    filled = 1 + factor_one * factor_two // TILE_CAP
    busiest = jax.random.randint(key_full, (), 0, N_ROW * N_COL)
    filled = filled.at[busiest].set(TILE_CAP)
    return filled.reshape(N_ROW, N_COL).astype(jnp.int32)


def draw_target_self(key, part):
    key = jax.random.fold_in(key, 37)
    chosen = jax.random.permutation(key, SRC_NODES)[:DST_NODES]
    return chosen.reshape(N_COL, DST_BLOCK).astype(jnp.int32)


def block_scale(stream_key, shape, cuts, smallest, top_value):
    factor_of = 1.0
    for axis_at, blocks in cuts:
        heights = jax.random.uniform(jax.random.fold_in(jax.random.fold_in(stream_key, 6), axis_at), (blocks,), jnp.float32, smallest / len(cuts), top_value / len(cuts))
        factor_of = factor_of * jnp.repeat(jnp.exp(heights), shape[axis_at] // blocks).reshape((-1,) + (1,) * (len(shape) - 1 - axis_at))
    return factor_of


def scatter_about(own_key, shape, width, limit, pieces=(), kind=jnp.bfloat16):
    array = width * jax.random.normal(own_key, shape, jnp.float32)
    if pieces:
        array = array * block_scale(own_key, shape, pieces, -0.22, 0.18)
    return jnp.clip(array, -limit, limit).astype(kind)


def setup_inputs(seed: int = 0) -> dict:
    splits = jax.random.split(jax.random.key(seed), 14)
    cotangent = scatter_about(splits[0], (N_COL, DST_BLOCK, HID), (DST_NODES // 2) ** -0.5, 0.125, ((0, 16), (1, 32)))
    preact_two = scatter_about(splits[1], (N_COL, DST_BLOCK, HID), 1.0, 6.0, ((0, 16), (1, 32)))
    aggregate_two = jnp.clip(2.0 * jax.random.uniform(splits[2], (N_COL, DST_BLOCK, HID), jnp.float32) ** block_scale(splits[2], (N_COL, DST_BLOCK, HID), ((0, 16), (1, 32)), -0.2, 0.2), 0.0, 2.0).astype(jnp.bfloat16)
    self_hidden = jnp.clip(2.0 * jax.random.uniform(splits[3], (N_COL, DST_BLOCK, HID), jnp.float32) ** block_scale(splits[3], (N_COL, DST_BLOCK, HID), ((0, 16), (1, 32)), -0.2, 0.2), 0.0, 2.0).astype(jnp.bfloat16)
    neigh_weight = scatter_about(splits[4], (HID, HID), HID ** -0.5, 0.375)
    root_weight = scatter_about(splits[5], (HID, HID), HID ** -0.5, 0.375)
    sampled_tiles = jnp.clip(0.049804688 * jax.random.uniform(splits[6], (N_ROW, N_COL, TILE_CAP, TILE, TILE), jnp.float32) ** block_scale(splits[6], (N_ROW, N_COL, TILE_CAP, TILE, TILE), ((0, 32), (1, 16)), -0.2, 0.2), 0.0, 0.049804688).astype(jnp.bfloat16)
    tile_slot = draw_tile_slot(jax.random.fold_in(splits[13], 71), 0)
    tile_count = draw_tile_count(jax.random.fold_in(splits[13], 71), 0)
    target_self = draw_target_self(jax.random.fold_in(splits[13], 71), 0)
    preact_one = scatter_about(splits[10], (N_ROW, SRC_BLOCK, HID), 1.0, 6.0, ((0, 32), (1, 16)))
    aggregate_one = scatter_about(splits[11], (N_ROW, SRC_BLOCK, FEAT), 1.0, 6.0, ((0, 32), (1, 16)))
    feature_one = scatter_about(splits[12], (N_ROW, SRC_BLOCK, FEAT), 1.0, 6.0, ((0, 32), (1, 16)))
    return {"cotangent": cotangent, "preact_two": preact_two, "aggregate_two": aggregate_two, "self_hidden": self_hidden, "neigh_weight": neigh_weight, "root_weight": root_weight, "sampled_tiles": sampled_tiles, "tile_slot": tile_slot, "tile_count": tile_count, "target_self": target_self, "preact_one": preact_one, "aggregate_one": aggregate_one, "feature_one": feature_one}


def reference(cotangent, preact_two, aggregate_two, self_hidden, neigh_weight, root_weight, sampled_tiles, tile_slot, tile_count, target_self, preact_one, aggregate_one, feature_one):
    contract_first = (((0,), (0,)), ((), ()))
    contract_last = (((1,), (1,)), ((), ()))
    delta_two = jnp.where(preact_two > 0, cotangent, jnp.zeros_like(cotangent)).reshape(DST_NODES, HID)
    neigh_term = lax.dot_general(aggregate_two.reshape(DST_NODES, HID), delta_two, contract_first, preferred_element_type=jnp.float32)
    root_term = lax.dot_general(self_hidden.reshape(DST_NODES, HID), delta_two, contract_first, preferred_element_type=jnp.float32)
    layer_two_grads = jnp.stack([neigh_term, root_term])
    message = lax.dot_general(delta_two, neigh_weight, contract_last, preferred_element_type=jnp.float32).astype(jnp.bfloat16)
    selfward = lax.dot_general(delta_two, root_weight, contract_last, preferred_element_type=jnp.float32).astype(jnp.bfloat16)
    message = message.reshape(N_COL, DST_TILES, TILE, HID)
    selfward = selfward.reshape(N_COL, DST_BLOCK, HID)

    def block_term(block_row, block_col):
        filled = tile_count[block_row, block_col]
        slot_numbers = tile_slot[block_row, block_col]
        alive_mask = (jnp.arange(TILE_CAP, dtype=jnp.int32) < filled).astype(jnp.float32)
        picked = message[block_col][slot_numbers // SRC_TILES].astype(jnp.float32)
        weights = sampled_tiles[block_row, block_col].astype(jnp.float32) * alive_mask[:, None, None]
        contrib = jnp.einsum("kij,kif->kjf", weights, picked)
        partial_value = jnp.zeros((SRC_TILES, TILE, HID), jnp.float32).at[slot_numbers % SRC_TILES].add(contrib)
        partial_value = partial_value.reshape(SRC_BLOCK, HID)
        local_row = target_self[block_col] - block_row * SRC_BLOCK
        target_row = jnp.where((local_row >= 0) & (local_row < SRC_BLOCK), local_row, SRC_BLOCK)
        partial_value = partial_value.at[target_row].add(selfward[block_col].astype(jnp.float32), mode="drop")
        rounded = lax.optimization_barrier(partial_value.astype(jnp.bfloat16))
        return rounded.astype(jnp.float32)

    def per_row(running, block_row):
        summed = lax.fori_loop(jnp.int32(0), jnp.int32(N_COL), lambda block_col, partial_sum: partial_sum + block_term(block_row, block_col), jnp.zeros((SRC_BLOCK, HID), jnp.float32))
        delta_one = jnp.where(preact_one[block_row] > 0, summed, jnp.zeros_like(summed)).astype(jnp.bfloat16)
        neigh_one = lax.dot_general(aggregate_one[block_row], delta_one, contract_first, preferred_element_type=jnp.float32)
        root_one = lax.dot_general(feature_one[block_row], delta_one, contract_first, preferred_element_type=jnp.float32)
        return (running[0] + neigh_one, running[1] + root_one), None

    start_value = (jnp.zeros((FEAT, HID), jnp.float32), jnp.zeros((FEAT, HID), jnp.float32))
    finished, unused = lax.scan(per_row, start_value, jnp.arange(N_ROW, dtype=jnp.int32))
    return layer_two_grads, jnp.stack([finished[0], finished[1]])
```

```python
import jax
import jax.numpy as jnp
from jax import lax
from jax.experimental import pallas as pl
from jax.experimental.pallas import tpu as pltpu
from jax.sharding import PartitionSpec as P

ROW = ("y", "zm", "zna", "znb")
COL = ("x", "zh", "core")
PAIRED_PLANE = ("znb", "y", "x")
VMEM = pl.BlockSpec(memory_space=pltpu.VMEM)
SMEM = pl.BlockSpec(memory_space=pltpu.SMEM)
HBM = pl.BlockSpec(memory_space=pltpu.HBM)
ANY = pl.BlockSpec(memory_space=pl.ANY)
ROWS_BOTH = (((0,), (0,)), ((), ()))
LAST_BOTH = (((1,), (1,)), ((), ()))


def exchange(blocks, axes):
    return lax.all_to_all(blocks, axes, 0, 0, tiled=True)


def spread(block, axes, n):
    return exchange(jnp.broadcast_to(block[None], (n,) + block.shape), axes)


def swap(value, axis):
    return lax.ppermute(value, axis, [(0, 1), (1, 0)])


def dot(left, right, dims=(((1,), (0,)), ((), ()))):
    return lax.dot_general(left, right, dims, preferred_element_type=jnp.float32)


def fetch(pairs, sems):
    copies = [pltpu.make_async_copy(source, target, sems.at[at]) for at, (source, target) in enumerate(pairs)]
    for copy in copies:
        copy.start()
    return copies


def mask_kernel(cot_ref, preact_ref, copies_ref, held, sems):
    for copy in fetch([(cot_ref, held.at[0]), (preact_ref, held.at[1])], sems):
        copy.wait()
    delta = masked(held[0], held[1])
    for at in range(copies_ref.shape[0]):
        copies_ref[at] = delta


def masked(value, preact):
    return jnp.where(preact.astype(jnp.float32) > 0, value.astype(jnp.float32), 0.0).astype(jnp.bfloat16)


def layout_kernel(slot_ref, count_ref, tiles_ref, target_ref, neigh_ref, root_ref, layout_ref, weight_ref):
    base = lax.axis_index(ROW) * 2048
    target = target_ref[...] - base
    layout_ref[:, :, :256] = jnp.zeros((16, 128, 256), jnp.bfloat16)
    for at in range(16):
        rows = lax.broadcasted_iota(jnp.int32, (128, 256), 0) + at * 128
        layout_ref[at, :, 256:] = jnp.where(rows == target, 1.0, 0.0).astype(jnp.bfloat16)
    weight_ref[0] = neigh_ref[...]
    weight_ref[1] = root_ref[...]
    count = count_ref[0, 0]
    for k in range(16):
        slot = slot_ref[0, k]
        for t in range(2):

            @pl.when((k < count) & (slot // 16 == t))
            def _():
                layout_ref[slot % 16, :, t * 128 : (t + 1) * 128] = tiles_ref[k].T


def bundle_kernel(agg_one_ref, feat_one_ref, preact_ref, cot_ref, pre_two_ref, agg_two_ref, self_ref, bundle_ref):
    bundle_ref[:128, :768] = agg_one_ref[...]
    bundle_ref[:128, 768:1536] = feat_one_ref[...]
    bundle_ref[:128, 1536:] = preact_ref[...]
    for at, ref in enumerate((cot_ref, pre_two_ref, agg_two_ref, self_ref)):
        padded = jnp.concatenate([ref[...].astype(jnp.float32), jnp.zeros((8, 256), jnp.float32)])
        bundle_ref[128:, at * 256 : (at + 1) * 256] = padded.astype(jnp.bfloat16)
    bundle_ref[128:, 1024:] = jnp.zeros((16, 768), jnp.bfloat16)


def by_core(body):
    core = lax.axis_index("core")
    for at in range(2):
        pl.when(core == at)(lambda at=at: body(at, slice(at * 128, at * 128 + 128), slice(128 - at * 128, 256 - at * 128)))


def turn_kernel(own_ref, recv_ref, turned_ref, preact_ref, two_ref):
    def body(core, mine, other):
        preact = slice(1536 + core * 128, 1664 + core * 128)
        two = [0.0, 0.0]
        for ref, rows in ((own_ref, mine), (recv_ref, other)):
            turned_ref[:, rows] = ref[:128, :1536].T
            preact_ref[rows] = ref[:128, preact]
            delta = masked(ref[128:, mine], ref[128:, 256 + core * 128 : 384 + core * 128])
            two[0] += dot(ref[128:, 512:768], delta, ROWS_BOTH)
            two[1] += dot(ref[128:, 768:1024], delta, ROWS_BOTH)
        two_ref[:256] = two[0].astype(jnp.bfloat16)
        two_ref[256:] = two[1].astype(jnp.bfloat16)

    by_core(body)


def product(delta_ref, weight_ref, layout_ref, columns):
    delta = delta_ref[...]
    message = [dot(delta, weight_ref[at, columns], LAST_BOTH).astype(jnp.bfloat16) for at in range(2)]
    return dot(layout_ref[...], jnp.concatenate(message))


def send_kernel(delta_ref, weight_ref, layout_ref, send_ref):
    def body(core, mine, other):
        send_ref[...] = product(delta_ref, weight_ref, layout_ref, other).astype(jnp.bfloat16)

    by_core(body)


def keep_kernel(delta_ref, weight_ref, layout_ref, keep_ref):
    def body(core, mine, other):
        keep_ref[...] = product(delta_ref, weight_ref, layout_ref, mine)

    by_core(body)


def pair_kernel(keep_ref, recv_ref, sum_ref):
    sum_ref[...] = (keep_ref[...] + recv_ref[...].astype(jnp.float32)).astype(jnp.bfloat16)


def terms_kernel(keep_ref, recv_ref, preact_ref, turned_ref, two_ref, terms_ref):
    delta = masked(keep_ref[...] + recv_ref[...].astype(jnp.float32), preact_ref[...])
    terms_ref[:1536] = dot(turned_ref[...], delta).astype(jnp.bfloat16)
    terms_ref[1536:] = two_ref[...]


def widen_half(half, value_ref, two_ref, one_ref, wide, sems):
    columns = pl.ds(pl.multiple_of(half * 128, 128), 128)
    copies = []
    for turn in range(4):
        rows = pl.ds(turn * 512, 512)
        target = one_ref.at[rows, columns] if turn < 3 else two_ref.at[:, columns]
        copies.append(pltpu.make_async_copy(wide.at[rows], target, sems.at[turn]))
        wide[rows] = value_ref[rows].astype(jnp.float32)
        copies[-1].start()
    for copy in copies:
        copy.wait()


def widen_own_kernel(own_ref, two_ref, one_ref, wide, sems):
    widen_half(lax.axis_index("core"), own_ref, two_ref, one_ref, wide, sems)


def widen_recv_kernel(recv_ref, two_in, one_in, two_ref, one_ref, wide, sems):
    widen_half(1 - lax.axis_index("core"), recv_ref, two_ref, one_ref, wide, sems)


def shape(dims, kind=jnp.bfloat16):
    return jax.ShapeDtypeStruct(dims, kind)


def call(kernel, outs, ins, *operands, flops=1_000_000, moved=1_000_000, vmem=16, **rest):
    return pl.pallas_call(
        kernel,
        out_shape=outs,
        in_specs=ins,
        compiler_params=pltpu.CompilerParams(vmem_limit_bytes=vmem * 2**20),
        cost_estimate=pl.CostEstimate(flops=flops, bytes_accessed=moved, transcendentals=0),
        name=kernel.__name__.replace("_kernel", ""),
        **rest,
    )(*operands)


def local(
    cotangent,
    preact_two,
    aggregate_two,
    self_hidden,
    neigh_weight,
    root_weight,
    sampled_tiles,
    tile_slot,
    tile_count,
    target_self,
    preact_one,
    aggregate_one,
    feature_one,
):
    zh = lax.axis_index("zh")
    copies = call(
        mask_kernel,
        shape((32, 8, 256)),
        [HBM] * 2,
        cotangent[0],
        preact_two[0],
        flops=10_000,
        moved=140_000,
        vmem=60,
        out_specs=VMEM,
        scratch_shapes=[pltpu.VMEM((2, 8, 256), jnp.bfloat16), pltpu.SemaphoreType.DMA((2,))],
    )
    gathered = exchange(copies, ROW).reshape(256, 256)
    layout, weight = call(
        layout_kernel,
        (shape((16, 128, 512)), shape((2, 256, 256))),
        [SMEM] * 2 + [VMEM] * 4,
        tile_slot[0],
        tile_count,
        sampled_tiles[0, 0],
        target_self,
        neigh_weight,
        root_weight,
        moved=3_000_000,
        out_specs=(VMEM, VMEM),
    )
    layout = layout.reshape(2048, 512)
    send = call(send_kernel, shape((2048, 128)), [VMEM] * 3, gathered, weight, layout, flops=300_000_000, out_specs=VMEM)
    recv = swap(send, "core")
    keep = call(
        keep_kernel,
        shape((2048, 128), jnp.float32),
        [VMEM] * 3,
        gathered,
        weight,
        layout,
        flops=300_000_000,
        moved=3_000_000,
        out_specs=VMEM,
    )
    blocks = call(pair_kernel, shape((2048, 128)), [VMEM] * 2, keep, recv, out_specs=VMEM)
    late = (aggregate_one, feature_one, preact_one, cotangent, preact_two, aggregate_two, self_hidden)
    blocks, late = lax.optimization_barrier((blocks, late))
    bundle = call(
        bundle_kernel,
        shape((144, 1792)),
        [VMEM] * 7,
        *(value[0] for value in late),
        out_specs=VMEM,
    )
    turned, preact, two_terms = call(
        turn_kernel,
        (shape((1536, 256)), shape((256, 128)), shape((512, 128))),
        [VMEM] * 2,
        bundle,
        swap(bundle, "core"),
        moved=2_000_000,
        out_specs=(VMEM,) * 3,
    )
    blocks = exchange(blocks.reshape(4, 2, 256, 128), ("x",)).astype(jnp.float32).sum(0)
    keep = lax.dynamic_index_in_dim(blocks, zh, 0, keepdims=False)
    send = lax.dynamic_index_in_dim(blocks, 1 - zh, 0, keepdims=False).astype(jnp.bfloat16)
    terms = call(
        terms_kernel,
        shape((2048, 128)),
        [VMEM] * 5,
        keep,
        swap(send, "zh"),
        preact,
        turned,
        two_terms,
        flops=100_000_000,
        out_specs=VMEM,
    )
    terms = exchange(terms.reshape(32, 64, 128), PAIRED_PLANE).astype(jnp.float32).sum(0)
    terms = spread(terms.astype(jnp.bfloat16), ("zna", "zm", "zh"), 8).astype(jnp.float32).sum(0)
    terms = spread(terms.astype(jnp.bfloat16), PAIRED_PLANE, 32).reshape(2048, 128)
    recv = swap(terms, "core")
    outs = (shape((512, 256), jnp.float32), shape((1536, 256), jnp.float32))
    scratch = [pltpu.VMEM((2048, 128), jnp.float32), pltpu.SemaphoreType.DMA((4,))]
    layer_two, layer_one = call(widen_own_kernel, outs, [VMEM], terms, out_specs=(ANY, ANY), scratch_shapes=scratch)
    layer_two, layer_one = call(
        widen_recv_kernel,
        outs,
        [VMEM, ANY, ANY],
        recv,
        layer_two,
        layer_one,
        out_specs=(ANY, ANY),
        scratch_shapes=scratch,
        input_output_aliases={1: 0, 2: 1},
    )
    return layer_two.reshape(2, 256, 256), layer_one.reshape(2, 768, 256)


def solution(mesh):
    fine = jax.sharding.Mesh(mesh.devices.reshape(4, 2, 2, 2, 4, 2, 2), ROW + COL)
    row, col = ROW, COL
    in_specs = (
        P(col, row, None),
        P(col, row, None),
        P(col, row, None),
        P(col, row, None),
        P(),
        P(),
        P(row, col, None, None, None),
        P(row, col, None),
        P(row, col),
        P(col, None),
        P(row, col, None),
        P(row, col, None),
        P(row, col, None),
    )
    out_specs = (P(), P())
    return jax.shard_map(local, mesh=fine, in_specs=in_specs, out_specs=out_specs, check_vma=False)
```

```python
import jax
import jax.numpy as jnp
from jax import lax
from jax.experimental import pallas as pl
from jax.experimental.pallas import tpu as pltpu
from jax.sharding import PartitionSpec as P

ROW = ("y", "zm", "zna", "znb")
COL = ("x", "zh", "core")
PAIRED_PLANE = ("znb", "y", "x")
VMEM = pl.BlockSpec(memory_space=pltpu.VMEM)
SMEM = pl.BlockSpec(memory_space=pltpu.SMEM)
HBM = pl.BlockSpec(memory_space=pltpu.HBM)
ANY = pl.BlockSpec(memory_space=pl.ANY)
ROWS_BOTH = (((0,), (0,)), ((), ()))
LAST_BOTH = (((1,), (1,)), ((), ()))


def exchange(blocks, axes):
    return lax.all_to_all(blocks, axes, 0, 0, tiled=True)


def spread(block, axes, n):
    return exchange(jnp.broadcast_to(block[None], (n,) + block.shape), axes)


def swap(value, axis):
    return lax.ppermute(value, axis, [(0, 1), (1, 0)])


def dot(left, right, dims=(((1,), (0,)), ((), ()))):
    return lax.dot_general(left, right, dims, preferred_element_type=jnp.float32)


def fetch(pairs, sems):
    copies = [pltpu.make_async_copy(source, target, sems.at[at]) for at, (source, target) in enumerate(pairs)]
    for copy in copies:
        copy.start()
    return copies


def mask_kernel(cot_ref, preact_ref, copies_ref, held, sems):
    for copy in fetch([(cot_ref, held.at[0]), (preact_ref, held.at[1])], sems):
        copy.wait()
    delta = masked(held[0], held[1])
    for at in range(copies_ref.shape[0]):
        copies_ref[at] = delta


def masked(value, preact):
    return jnp.where(preact.astype(jnp.float32) > 0, value.astype(jnp.float32), 0.0).astype(jnp.bfloat16)


def layout_kernel(slot_ref, count_ref, tiles_ref, target_ref, neigh_ref, root_ref, layout_ref, weight_ref):
    base = lax.axis_index(ROW) * 2048
    target = target_ref[...] - base
    layout_ref[:, :, :256] = jnp.zeros((16, 128, 256), jnp.bfloat16)
    for at in range(16):
        rows = lax.broadcasted_iota(jnp.int32, (128, 256), 0) + at * 128
        layout_ref[at, :, 256:] = jnp.where(rows == target, 1.0, 0.0).astype(jnp.bfloat16)
    weight_ref[0] = neigh_ref[...]
    weight_ref[1] = root_ref[...]
    count = count_ref[0, 0]
    for k in range(16):
        slot = slot_ref[0, k]
        for t in range(2):

            @pl.when((k < count) & (slot // 16 == t))
            def _():
                layout_ref[slot % 16, :, t * 128 : (t + 1) * 128] = tiles_ref[k].T


def bundle_kernel(agg_one_ref, feat_one_ref, preact_ref, cot_ref, pre_two_ref, agg_two_ref, self_ref, bundle_ref):
    bundle_ref[:128, :768] = agg_one_ref[...]
    bundle_ref[:128, 768:1536] = feat_one_ref[...]
    bundle_ref[:128, 1536:] = preact_ref[...]
    for at, ref in enumerate((cot_ref, pre_two_ref, agg_two_ref, self_ref)):
        padded = jnp.concatenate([ref[...].astype(jnp.float32), jnp.zeros((8, 256), jnp.float32)])
        bundle_ref[128:, at * 256 : (at + 1) * 256] = padded.astype(jnp.bfloat16)
    bundle_ref[128:, 1024:] = jnp.zeros((16, 768), jnp.bfloat16)


def by_core(body):
    core = lax.axis_index("core")
    for at in range(2):
        pl.when(core == at)(lambda at=at: body(at, slice(at * 128, at * 128 + 128), slice(128 - at * 128, 256 - at * 128)))


def turn_kernel(own_ref, recv_ref, turned_ref, preact_ref, two_ref):
    def body(core, mine, other):
        preact = slice(1536 + core * 128, 1664 + core * 128)
        two = [0.0, 0.0]
        for ref, rows in ((own_ref, mine), (recv_ref, other)):
            turned_ref[:, rows] = ref[:128, :1536].T
            preact_ref[rows] = ref[:128, preact]
            delta = masked(ref[128:, mine], ref[128:, 256 + core * 128 : 384 + core * 128])
            two[0] += dot(ref[128:, 512:768], delta, ROWS_BOTH)
            two[1] += dot(ref[128:, 768:1024], delta, ROWS_BOTH)
        two_ref[:256] = two[0].astype(jnp.bfloat16)
        two_ref[256:] = two[1].astype(jnp.bfloat16)

    by_core(body)


def by_rows(start, count, body, step=128):
    @pl.loop(0, count // step)
    def _(turn):
        body(pl.ds(pl.multiple_of(start + turn * step, step), step))


def product(delta_ref, weight_ref, layout_ref, columns):
    delta = delta_ref[...]
    message = [dot(delta, weight_ref[at, columns], LAST_BOTH).astype(jnp.bfloat16) for at in range(2)]
    return dot(layout_ref[...], jnp.concatenate(message))


def send_kernel(delta_ref, weight_ref, layout_ref, send_ref):
    def body(core, mine, other):
        send_ref[...] = product(delta_ref, weight_ref, layout_ref, other).astype(jnp.bfloat16)

    by_core(body)


def keep_kernel(delta_ref, weight_ref, layout_ref, keep_ref):
    def body(core, mine, other):
        keep_ref[...] = product(delta_ref, weight_ref, layout_ref, mine)

    by_core(body)


def pair_kernel(keep_ref, recv_ref, sum_ref):
    def add(rows):
        sum_ref[rows] = (keep_ref[rows] + recv_ref[rows].astype(jnp.float32)).astype(jnp.bfloat16)

    by_rows(0, 2048, add)


def terms_kernel(keep_ref, recv_ref, preact_ref, turned_ref, two_ref, terms_ref):
    delta = masked(keep_ref[...] + recv_ref[...].astype(jnp.float32), preact_ref[...])
    terms_ref[:1536] = dot(turned_ref[...], delta).astype(jnp.bfloat16)
    terms_ref[1536:] = two_ref[...]


def widen_half(half, value_ref, two_ref, one_ref, wide, sems):
    columns = pl.ds(pl.multiple_of(half * 128, 128), 128)
    copies = []
    for turn in range(4):
        rows = pl.ds(turn * 512, 512)
        target = one_ref.at[rows, columns] if turn < 3 else two_ref.at[:, columns]
        copies.append(pltpu.make_async_copy(wide.at[rows], target, sems.at[turn]))

        def convert(part):
            wide[part] = value_ref[part].astype(jnp.float32)

        by_rows(turn * 512, 512, convert)
        copies[-1].start()
    for copy in copies:
        copy.wait()


def widen_own_kernel(own_ref, two_ref, one_ref, wide, sems):
    widen_half(lax.axis_index("core"), own_ref, two_ref, one_ref, wide, sems)


def widen_recv_kernel(recv_ref, two_in, one_in, two_ref, one_ref, wide, sems):
    widen_half(1 - lax.axis_index("core"), recv_ref, two_ref, one_ref, wide, sems)


def shape(dims, kind=jnp.bfloat16):
    return jax.ShapeDtypeStruct(dims, kind)


def call(kernel, outs, ins, *operands, flops=1_000_000, moved=1_000_000, vmem=16, **rest):
    return pl.pallas_call(
        kernel,
        out_shape=outs,
        in_specs=ins,
        compiler_params=pltpu.CompilerParams(vmem_limit_bytes=vmem * 2**20),
        cost_estimate=pl.CostEstimate(flops=flops, bytes_accessed=moved, transcendentals=0),
        name=kernel.__name__.replace("_kernel", ""),
        **rest,
    )(*operands)


def local(
    cotangent,
    preact_two,
    aggregate_two,
    self_hidden,
    neigh_weight,
    root_weight,
    sampled_tiles,
    tile_slot,
    tile_count,
    target_self,
    preact_one,
    aggregate_one,
    feature_one,
):
    zh = lax.axis_index("zh")
    copies = call(
        mask_kernel,
        shape((32, 8, 256)),
        [HBM] * 2,
        cotangent[0],
        preact_two[0],
        flops=10_000,
        moved=140_000,
        vmem=60,
        out_specs=VMEM,
        scratch_shapes=[pltpu.VMEM((2, 8, 256), jnp.bfloat16), pltpu.SemaphoreType.DMA((2,))],
    )
    gathered = exchange(copies, ROW).reshape(256, 256)
    layout, weight = call(
        layout_kernel,
        (shape((16, 128, 512)), shape((2, 256, 256))),
        [SMEM] * 2 + [VMEM] * 4,
        tile_slot[0],
        tile_count,
        sampled_tiles[0, 0],
        target_self,
        neigh_weight,
        root_weight,
        moved=3_000_000,
        out_specs=(VMEM, VMEM),
    )
    layout = layout.reshape(2048, 512)
    send = call(send_kernel, shape((2048, 128)), [VMEM] * 3, gathered, weight, layout, flops=300_000_000, out_specs=VMEM)
    recv = swap(send, "core")
    keep = call(
        keep_kernel,
        shape((2048, 128), jnp.float32),
        [VMEM] * 3,
        gathered,
        weight,
        layout,
        flops=300_000_000,
        moved=3_000_000,
        out_specs=VMEM,
    )
    blocks = call(pair_kernel, shape((2048, 128)), [VMEM] * 2, keep, recv, out_specs=VMEM)
    late = (aggregate_one, feature_one, preact_one, cotangent, preact_two, aggregate_two, self_hidden)
    blocks, late = lax.optimization_barrier((blocks, late))
    bundle = call(
        bundle_kernel,
        shape((144, 1792)),
        [VMEM] * 7,
        *(value[0] for value in late),
        out_specs=VMEM,
    )
    turned, preact, two_terms = call(
        turn_kernel,
        (shape((1536, 256)), shape((256, 128)), shape((512, 128))),
        [VMEM] * 2,
        bundle,
        swap(bundle, "core"),
        moved=2_000_000,
        out_specs=(VMEM,) * 3,
    )
    blocks = exchange(blocks.reshape(4, 2, 256, 128), ("x",)).astype(jnp.float32).sum(0)
    keep = lax.dynamic_index_in_dim(blocks, zh, 0, keepdims=False)
    send = lax.dynamic_index_in_dim(blocks, 1 - zh, 0, keepdims=False).astype(jnp.bfloat16)
    terms = call(
        terms_kernel,
        shape((2048, 128)),
        [VMEM] * 5,
        keep,
        swap(send, "zh"),
        preact,
        turned,
        two_terms,
        flops=100_000_000,
        out_specs=VMEM,
    )
    terms = exchange(terms.reshape(32, 64, 128), PAIRED_PLANE).astype(jnp.float32).sum(0)
    terms = spread(terms.astype(jnp.bfloat16), ("zna", "zm", "zh"), 8).astype(jnp.float32).sum(0)
    terms = spread(terms.astype(jnp.bfloat16), PAIRED_PLANE, 32).reshape(2048, 128)
    recv = swap(terms, "core")
    outs = (shape((512, 256), jnp.float32), shape((1536, 256), jnp.float32))
    scratch = [pltpu.VMEM((2048, 128), jnp.float32), pltpu.SemaphoreType.DMA((4,))]
    layer_two, layer_one = call(widen_own_kernel, outs, [VMEM], terms, out_specs=(ANY, ANY), scratch_shapes=scratch)
    layer_two, layer_one = call(
        widen_recv_kernel,
        outs,
        [VMEM, ANY, ANY],
        recv,
        layer_two,
        layer_one,
        out_specs=(ANY, ANY),
        scratch_shapes=scratch,
        input_output_aliases={1: 0, 2: 1},
    )
    return layer_two.reshape(2, 256, 256), layer_one.reshape(2, 768, 256)


def solution(mesh):
    fine = jax.sharding.Mesh(mesh.devices.reshape(4, 2, 2, 2, 4, 2, 2), ROW + COL)
    row, col = ROW, COL
    in_specs = (
        P(col, row, None),
        P(col, row, None),
        P(col, row, None),
        P(col, row, None),
        P(),
        P(),
        P(row, col, None, None, None),
        P(row, col, None),
        P(row, col),
        P(col, None),
        P(row, col, None),
        P(row, col, None),
        P(row, col, None),
    )
    out_specs = (P(), P())
    return jax.shard_map(local, mesh=fine, in_specs=in_specs, out_specs=out_specs, check_vma=False)
```

```python
import jax
import jax.numpy as jnp
from jax import lax
from jax.experimental import pallas as pl
from jax.experimental.pallas import tpu as pltpu
from jax.sharding import PartitionSpec as P

ROW = ("y", "zm", "zna", "znb")
COL = ("x", "zh", "core")
PAIRED_PLANE = ("znb", "y", "x")
VMEM = pl.BlockSpec(memory_space=pltpu.VMEM)
SMEM = pl.BlockSpec(memory_space=pltpu.SMEM)
HBM = pl.BlockSpec(memory_space=pltpu.HBM)
ANY = pl.BlockSpec(memory_space=pl.ANY)
ROWS_BOTH = (((0,), (0,)), ((), ()))
LAST_BOTH = (((1,), (1,)), ((), ()))


def exchange(blocks, axes):
    return lax.all_to_all(blocks, axes, 0, 0, tiled=True)


def spread(block, axes, n):
    return exchange(jnp.broadcast_to(block[None], (n,) + block.shape), axes)


def swap(value, axis):
    return lax.ppermute(value, axis, [(0, 1), (1, 0)])


def dot(left, right, dims=(((1,), (0,)), ((), ()))):
    return lax.dot_general(left, right, dims, preferred_element_type=jnp.float32)


def fetch(pairs, sems):
    copies = [pltpu.make_async_copy(source, target, sems.at[at]) for at, (source, target) in enumerate(pairs)]
    for copy in copies:
        copy.start()
    return copies


def mask_kernel(cot_ref, preact_ref, copies_ref, held, sems):
    for copy in fetch([(cot_ref, held.at[0]), (preact_ref, held.at[1])], sems):
        copy.wait()
    delta = masked(held[0], held[1])
    for at in range(copies_ref.shape[0]):
        copies_ref[at] = delta


def masked(value, preact):
    return jnp.where(preact.astype(jnp.float32) > 0, value.astype(jnp.float32), 0.0).astype(jnp.bfloat16)


def layout_kernel(slot_ref, count_ref, tiles_ref, target_ref, neigh_ref, root_ref, layout_ref, weight_ref):
    base = lax.axis_index(ROW) * 2048
    target = target_ref[...] - base
    layout_ref[:, :, :256] = jnp.zeros((16, 128, 256), jnp.bfloat16)
    for at in range(16):
        rows = lax.broadcasted_iota(jnp.int32, (128, 256), 0) + at * 128
        layout_ref[at, :, 256:] = jnp.where(rows == target, 1.0, 0.0).astype(jnp.bfloat16)
    weight_ref[0] = neigh_ref[...]
    weight_ref[1] = root_ref[...]
    count = count_ref[0, 0]
    for k in range(16):
        slot = slot_ref[0, k]
        for t in range(2):

            @pl.when((k < count) & (slot // 16 == t))
            def _():
                layout_ref[slot % 16, :, t * 128 : (t + 1) * 128] = tiles_ref[k].T


def bundle_kernel(agg_one_ref, feat_one_ref, preact_ref, cot_ref, pre_two_ref, agg_two_ref, self_ref, bundle_ref):
    bundle_ref[:128, :768] = agg_one_ref[...]
    bundle_ref[:128, 768:1536] = feat_one_ref[...]
    bundle_ref[:128, 1536:] = preact_ref[...]
    for at, ref in enumerate((cot_ref, pre_two_ref, agg_two_ref, self_ref)):
        padded = jnp.concatenate([ref[...].astype(jnp.float32), jnp.zeros((8, 256), jnp.float32)])
        bundle_ref[128:, at * 256 : (at + 1) * 256] = padded.astype(jnp.bfloat16)
    bundle_ref[128:, 1024:] = jnp.zeros((16, 768), jnp.bfloat16)


def by_core(body):
    core = lax.axis_index("core")
    for at in range(2):
        pl.when(core == at)(lambda at=at: body(at, slice(at * 128, at * 128 + 128), slice(128 - at * 128, 256 - at * 128)))


def turn_kernel(own_ref, recv_ref, turned_ref, preact_ref, two_ref):
    def body(core, mine, other):
        preact = slice(1536 + core * 128, 1664 + core * 128)
        two = [0.0, 0.0]
        for ref, rows in ((own_ref, mine), (recv_ref, other)):
            turned_ref[:, rows] = ref[:128, :1536].T
            preact_ref[rows] = ref[:128, preact]
            delta = masked(ref[128:, mine], ref[128:, 256 + core * 128 : 384 + core * 128])
            two[0] += dot(ref[128:, 512:768], delta, ROWS_BOTH)
            two[1] += dot(ref[128:, 768:1024], delta, ROWS_BOTH)
        two_ref[:256] = two[0].astype(jnp.bfloat16)
        two_ref[256:] = two[1].astype(jnp.bfloat16)

    by_core(body)


def by_rows(start, count, body, step=128):
    @pl.loop(0, count // step)
    def _(turn):
        body(pl.ds(pl.multiple_of(start + turn * step, step), step))


def natural_order():
    for row in range(32):
        y, zm, zna, znb = row // 8, row // 4 % 2, row // 2 % 2, row % 2
        yield ((y * 2 + znb) * 2 + zna) * 2 + zm


def product(delta_ref, weight_ref, layout_ref, columns):
    delta = jnp.concatenate([delta_ref[at].astype(jnp.float32) for at in natural_order()]).astype(jnp.bfloat16)
    message = [dot(delta, weight_ref[at, columns], LAST_BOTH).astype(jnp.bfloat16) for at in range(2)]
    return dot(layout_ref[...], jnp.concatenate(message))


def send_kernel(delta_ref, weight_ref, layout_ref, send_ref):
    def body(core, mine, other):
        send_ref[...] = product(delta_ref, weight_ref, layout_ref, other).astype(jnp.bfloat16)

    by_core(body)


def keep_kernel(delta_ref, weight_ref, layout_ref, keep_ref):
    def body(core, mine, other):
        keep_ref[...] = product(delta_ref, weight_ref, layout_ref, mine)

    by_core(body)


def pair_kernel(keep_ref, recv_ref, sum_ref):
    def add(rows):
        sum_ref[rows] = (keep_ref[rows] + recv_ref[rows].astype(jnp.float32)).astype(jnp.bfloat16)

    by_rows(0, 2048, add)


def terms_kernel(keep_ref, recv_ref, preact_ref, turned_ref, two_ref, terms_ref):
    delta = masked(keep_ref[...] + recv_ref[...].astype(jnp.float32), preact_ref[...])
    terms_ref[:1536] = dot(turned_ref[...], delta).astype(jnp.bfloat16)
    terms_ref[1536:] = two_ref[...]


def widen_half(half, value_ref, two_ref, one_ref, wide, sems):
    columns = pl.ds(pl.multiple_of(half * 128, 128), 128)
    copies = []
    for turn in range(4):
        rows = pl.ds(turn * 512, 512)
        target = one_ref.at[rows, columns] if turn < 3 else two_ref.at[:, columns]
        copies.append(pltpu.make_async_copy(wide.at[rows], target, sems.at[turn]))

        def convert(part):
            wide[part] = value_ref[part].astype(jnp.float32)

        by_rows(turn * 512, 512, convert)
        copies[-1].start()
    for copy in copies:
        copy.wait()


def widen_own_kernel(own_ref, two_ref, one_ref, wide, sems):
    widen_half(lax.axis_index("core"), own_ref, two_ref, one_ref, wide, sems)


def widen_recv_kernel(recv_ref, two_in, one_in, two_ref, one_ref, wide, sems):
    widen_half(1 - lax.axis_index("core"), recv_ref, two_ref, one_ref, wide, sems)


def shape(dims, kind=jnp.bfloat16):
    return jax.ShapeDtypeStruct(dims, kind)


def call(kernel, outs, ins, *operands, flops=1_000_000, moved=1_000_000, vmem=16, **rest):
    return pl.pallas_call(
        kernel,
        out_shape=outs,
        in_specs=ins,
        compiler_params=pltpu.CompilerParams(vmem_limit_bytes=vmem * 2**20),
        cost_estimate=pl.CostEstimate(flops=flops, bytes_accessed=moved, transcendentals=0),
        name=kernel.__name__.replace("_kernel", ""),
        **rest,
    )(*operands)


def local(
    cotangent,
    preact_two,
    aggregate_two,
    self_hidden,
    neigh_weight,
    root_weight,
    sampled_tiles,
    tile_slot,
    tile_count,
    target_self,
    preact_one,
    aggregate_one,
    feature_one,
):
    zh = lax.axis_index("zh")
    copies = call(
        mask_kernel,
        shape((32, 8, 256)),
        [HBM] * 2,
        cotangent[0],
        preact_two[0],
        flops=10_000,
        moved=140_000,
        vmem=60,
        out_specs=VMEM,
        scratch_shapes=[pltpu.VMEM((2, 8, 256), jnp.bfloat16), pltpu.SemaphoreType.DMA((2,))],
    )
    gathered = exchange(copies, ("y", "znb", "zna", "zm"))
    layout, weight = call(
        layout_kernel,
        (shape((16, 128, 512)), shape((2, 256, 256))),
        [SMEM] * 2 + [VMEM] * 4,
        tile_slot[0],
        tile_count,
        sampled_tiles[0, 0],
        target_self,
        neigh_weight,
        root_weight,
        moved=3_000_000,
        out_specs=(VMEM, VMEM),
    )
    layout = layout.reshape(2048, 512)
    send = call(send_kernel, shape((2048, 128)), [VMEM] * 3, gathered, weight, layout, flops=300_000_000, out_specs=VMEM)
    recv = swap(send, "core")
    keep = call(
        keep_kernel,
        shape((2048, 128), jnp.float32),
        [VMEM] * 3,
        gathered,
        weight,
        layout,
        flops=300_000_000,
        moved=3_000_000,
        out_specs=VMEM,
    )
    blocks = call(pair_kernel, shape((2048, 128)), [VMEM] * 2, keep, recv, out_specs=VMEM)
    late = (aggregate_one, feature_one, preact_one, cotangent, preact_two, aggregate_two, self_hidden)
    blocks, late = lax.optimization_barrier((blocks, late))
    bundle = call(
        bundle_kernel,
        shape((144, 1792)),
        [VMEM] * 7,
        *(value[0] for value in late),
        out_specs=VMEM,
    )
    turned, preact, two_terms = call(
        turn_kernel,
        (shape((1536, 256)), shape((256, 128)), shape((512, 128))),
        [VMEM] * 2,
        bundle,
        swap(bundle, "core"),
        moved=2_000_000,
        out_specs=(VMEM,) * 3,
    )
    blocks = exchange(blocks.reshape(4, 2, 256, 128), ("x",)).astype(jnp.float32).sum(0)
    keep = lax.dynamic_index_in_dim(blocks, zh, 0, keepdims=False)
    send = lax.dynamic_index_in_dim(blocks, 1 - zh, 0, keepdims=False).astype(jnp.bfloat16)
    terms = call(
        terms_kernel,
        shape((2048, 128)),
        [VMEM] * 5,
        keep,
        swap(send, "zh"),
        preact,
        turned,
        two_terms,
        flops=100_000_000,
        out_specs=VMEM,
    )
    terms = exchange(terms.reshape(32, 64, 128), PAIRED_PLANE).astype(jnp.float32).sum(0)
    terms = spread(terms.astype(jnp.bfloat16), ("zna", "zm", "zh"), 8).astype(jnp.float32).sum(0)
    terms = spread(terms.astype(jnp.bfloat16), PAIRED_PLANE, 32).reshape(2048, 128)
    recv = swap(terms, "core")
    outs = (shape((512, 256), jnp.float32), shape((1536, 256), jnp.float32))
    scratch = [pltpu.VMEM((2048, 128), jnp.float32), pltpu.SemaphoreType.DMA((4,))]
    layer_two, layer_one = call(widen_own_kernel, outs, [VMEM], terms, out_specs=(ANY, ANY), scratch_shapes=scratch)
    layer_two, layer_one = call(
        widen_recv_kernel,
        outs,
        [VMEM, ANY, ANY],
        recv,
        layer_two,
        layer_one,
        out_specs=(ANY, ANY),
        scratch_shapes=scratch,
        input_output_aliases={1: 0, 2: 1},
    )
    return layer_two.reshape(2, 256, 256), layer_one.reshape(2, 768, 256)


def solution(mesh):
    fine = jax.sharding.Mesh(mesh.devices.reshape(4, 2, 2, 2, 4, 2, 2), ROW + COL)
    row, col = ROW, COL
    in_specs = (
        P(col, row, None),
        P(col, row, None),
        P(col, row, None),
        P(col, row, None),
        P(),
        P(),
        P(row, col, None, None, None),
        P(row, col, None),
        P(row, col),
        P(col, None),
        P(row, col, None),
        P(row, col, None),
        P(row, col, None),
    )
    out_specs = (P(), P())
    return jax.shard_map(local, mesh=fine, in_specs=in_specs, out_specs=out_specs, check_vma=False)
```
